32 devices in a mesh: rep: 2 (over core), exp: 16 (over z, y, x).
Axes of the slice: x: 2, y: 2, z: 4, core: 2. Of those that a mesh axis runs over, the one named last changes fastest.
Arguments:
- tokens: bfloat16 [25216, 768], P(('rep', 'exp')), may hold values from -6 to 6
- ln1_gain: bfloat16 [768], P('exp'), may hold values from 0.5 to 1.5
- ln1_bias: bfloat16 [768], P('exp'), may hold values from -1.25 to 1.25
- qkv_weight: bfloat16 [768, 2304], P('exp'), may hold values from -0.21875 to 0.21875
- out_weight: bfloat16 [768, 768], P('exp'), may hold values from -0.875 to 0.875
- ln2_gain: bfloat16 [768], P('exp'), may hold values from 0.5 to 1.5
- ln2_bias: bfloat16 [768], P('exp'), may hold values from -1.25 to 1.25
- router_weight: bfloat16 [768, 16], P('exp'), may hold values from -0.21875 to 0.21875
- expert_in: bfloat16 [16, 768, 3072], P('exp'), may hold values from -0.21875 to 0.21875
- expert_out: bfloat16 [16, 3072, 768], P('exp'), may hold values from -2.5 to 2.5
- expert_ids: int32 [25216, 2], P(('rep', 'exp')), may hold values from 0 to 15, as said below
- slot_ids: int32 [25216, 2], P(('rep', 'exp')), may hold values from 0 to 127, as said below
- dropped: int32 [25216, 2], P(('rep', 'exp')), may hold values from 0 to 1, as said below
- cotangent: bfloat16 [25216, 768], P(('rep', 'exp')), may hold values from -6 to 6
Outputs:
- mixed: bfloat16 [25216, 768], P(('rep', 'exp'))
- grad_tokens: float32 [25216, 768], P(('rep', 'exp'))
- grad_ln1_gain: float32 [768], P('exp')
- grad_ln1_bias: float32 [768], P('exp')
- grad_qkv: float32 [768, 2304], P('exp')
- grad_out_weight: float32 [768, 768], P('exp')
- grad_ln2_gain: float32 [768], P('exp')
- grad_ln2_bias: float32 [768], P('exp')
- grad_router: float32 [768, 16], P('exp')
- grad_expert_in: float32 [16, 768, 3072], P('exp')
- grad_expert_out: float32 [16, 3072, 768], P('exp')
The draws below stay inside these ranges and needn't reach their ends.
Inputs may be any that keep to these rules, and one draw needn't show every extreme that they name: `expert_ids`: each token names 2 different experts. `slot_ids`: slots count a device's earlier routes to the same expert, tokens in order and a token's routes in order; 0 where dropped; in the rows of each device some expert is named by more than 128 routes. `dropped`: 1 exactly where that count reaches 128.
All inputs are finite; a program needn't handle non-finite values.
Results may differ from the reference program's by a relative error of at most 0.018.
Values may be sent and summed in bfloat16 or wider, within the bound.
A program may use at most 256 MiB of HBM per device.

```python
import jax
import jax.numpy as jnp
from jax import lax

D = 768
HEADS = 12
HEAD = 64
FF = 3072
SEQ = 197
EXPERTS = 16
TOK_DEV = 788
TOKENS = 25216
CAP = 128


def routing(key):
    blocks = TOKENS // TOK_DEV
    key_hot, key_order, key_lead, key_other = jax.random.split(key, 4)
    hot_expert = jax.random.randint(key_hot, (blocks, 1), 0, EXPERTS)
    order_keys = jax.random.split(key_order, blocks)

    def block_order(one_key):
        return jax.random.permutation(one_key, TOK_DEV)
    ranking = jax.vmap(block_order)(order_keys)
    leading = jax.random.randint(key_lead, (blocks, TOK_DEV), 0, EXPERTS)
    leading = jnp.where(ranking < CAP + 1, hot_expert, leading)
    offset = jax.random.randint(key_other, (blocks, TOK_DEV), 1, EXPERTS)
    second = (leading + offset) % EXPERTS
    chosen = jnp.stack([leading, second], axis=-1).astype(jnp.int32)
    flat_ids = chosen.reshape(blocks, TOK_DEV * 2)
    onehot = (flat_ids[:, :, None] == jnp.arange(EXPERTS, dtype=jnp.int32)[None, None, :]).astype(jnp.int32)
    earlier = jnp.cumsum(onehot, axis=1) - onehot
    position = jnp.sum(earlier * onehot, axis=-1).reshape(blocks, TOK_DEV, 2)
    lost = (position >= CAP).astype(jnp.int32)
    position = jnp.where(lost == 1, 0, position).astype(jnp.int32)
    return (chosen.reshape(TOKENS, 2), position.reshape(TOKENS, 2), lost.reshape(TOKENS, 2))


def draw_expert_ids(key, part):
    shared = routing(key)
    return shared[0]


def draw_slot_ids(key, part):
    shared = routing(key)
    return shared[1]


def draw_dropped(key, part):
    shared = routing(key)
    return shared[2]


def levels(key, shape, cuts, least, largest):
    def one(dim, blocks):
        steps = jax.random.uniform(jax.random.fold_in(jax.random.fold_in(key, 6), dim), (blocks,), jnp.float32, least / len(cuts), largest / len(cuts))
        return jnp.repeat(jnp.exp(steps), shape[dim] // blocks).reshape((-1,) + (1,) * (len(shape) - dim - 1))

    level = one(*cuts[0])
    for cut in cuts[1:]:
        level = level * one(*cut)
    return level


def bell_draw(rng, dims, width, limit, pieces=(), held_as=jnp.bfloat16):
    level = levels(rng, dims, pieces, -0.22, 0.18) if pieces else 1.0
    array = jax.random.normal(rng, dims, jnp.float32) * width * level
    return jnp.minimum(jnp.maximum(array, -limit), limit).astype(held_as)


def setup_inputs(seed: int = 0) -> dict:
    keys = jax.random.split(jax.random.key(seed), 15)
    return {
        "tokens": bell_draw(keys[0], (TOKENS, D), 1.0, 6.0, ((0, 32),)),
        "ln1_gain": jnp.clip(1.0 + 0.1 * jax.random.normal(keys[1], (D,), jnp.float32), 0.5, 1.5).astype(jnp.bfloat16),
        "ln1_bias": bell_draw(keys[2], (D,), 0.2, 1.25, ((0, 16),)),
        "qkv_weight": bell_draw(keys[3], (D, 3 * D), D ** -0.5, 0.21875, ((0, 16),)),
        "out_weight": bell_draw(keys[4], (D, D), (D // 16) ** -0.5, 0.875, ((0, 16),)),
        "ln2_gain": jnp.clip(1.0 + 0.1 * jax.random.normal(keys[5], (D,), jnp.float32), 0.5, 1.5).astype(jnp.bfloat16),
        "ln2_bias": bell_draw(keys[6], (D,), 0.2, 1.25, ((0, 16),)),
        "router_weight": bell_draw(keys[7], (D, EXPERTS), D ** -0.5, 0.21875, ((0, 16),)),
        "expert_in": bell_draw(keys[8], (EXPERTS, D, FF), D ** -0.5, 0.21875, ((0, 16),)),
        "expert_out": bell_draw(keys[9], (EXPERTS, FF, D), (max(FF // 512, 1)) ** -0.5, 2.5, ((0, 16),)),
        "expert_ids": draw_expert_ids(jax.random.fold_in(keys[14], 71), 0),
        "slot_ids": draw_slot_ids(jax.random.fold_in(keys[14], 71), 0),
        "dropped": draw_dropped(jax.random.fold_in(keys[14], 71), 0),
        "cotangent": bell_draw(keys[13], (TOKENS, D), 1.0, 6.0, ((0, 32),)),
    }


@jax.custom_vjp
def low(v):
    return lax.optimization_barrier(v.astype(jnp.bfloat16)).astype(jnp.float32)

@jax.custom_vjp
def low_back(v):
    return v

def low_keep(v):
    return (low(v), None)

def low_pass(kept, grad):
    return (grad,)

def back_keep(v):
    return (v, None)

def back_low(kept, grad):
    return (low(grad),)
low.defvjp(low_keep, low_pass)
low_back.defvjp(back_keep, back_low)
epsilon = 1e-06
highest = lax.Precision.HIGHEST

def layer_norm(values, gain, offset):
    centre = lax.optimization_barrier(jnp.mean(values, axis=-1, keepdims=True))
    centred = values - centre
    spread = lax.optimization_barrier(jnp.mean(centred * centred, axis=-1, keepdims=True))
    return centred * lax.rsqrt(spread + epsilon) * gain + offset

def reference(tokens, ln1_gain, ln1_bias, qkv_weight, out_weight, ln2_gain, ln2_bias, router_weight, expert_in, expert_out, expert_ids, slot_ids, dropped, cotangent):
    n_images = TOKENS // SEQ
    scale = HEAD ** (-0.5)
    slot_count = TOKENS // TOK_DEV * CAP
    blocks_of = jnp.arange(TOKENS, dtype=jnp.int32) // TOK_DEV
    flat_slots = (blocks_of[:, None] * CAP + slot_ids).astype(jnp.int32)
    keep_mask = dropped == 0
    onehot = (expert_ids[:, :, None] == jnp.arange(EXPERTS, dtype=jnp.int32)[None, None, :]).astype(jnp.float32)

    def one_image(parts):
        queries, keys_all, values_all = parts
        scores = low_back(jnp.einsum('qhd,khd->hqk', queries, keys_all, precision=highest) * scale)
        weights = jax.nn.softmax(scores, axis=-1)
        return jnp.einsum('hqk,khd->qhd', low(weights), values_all, precision=highest)

    def forward(inputs, gain_one, bias_one, w_qkv, w_attn, gain_two, bias_two, w_router, w_first, w_second):
        normed1 = low(layer_norm(inputs, gain_one, bias_one))
        qkv = low(low_back(jnp.dot(normed1, w_qkv, precision=highest)))
        queries = qkv[:, :D].reshape(n_images, SEQ, HEADS, HEAD)
        keys_all = qkv[:, D:2 * D].reshape(n_images, SEQ, HEADS, HEAD)
        values_all = qkv[:, 2 * D:].reshape(n_images, SEQ, HEADS, HEAD)
        attended = lax.map(jax.checkpoint(one_image), (queries, keys_all, values_all))
        attended = low(low_back(attended.reshape(TOKENS, D)))
        mid = inputs + low_back(jnp.dot(attended, w_attn, precision=highest))
        normed2 = low(layer_norm(mid, gain_two, bias_two))
        logits = low_back(jnp.dot(normed2, w_router, precision=highest))
        router_probs = jax.nn.softmax(logits, axis=-1)
        gates = lax.optimization_barrier(jnp.sum(onehot * router_probs[:, None, :], axis=-1)) * keep_mask.astype(jnp.float32)

        def expert_step(total, item):
            index, first_w, second_w = item
            chosen = (expert_ids == index) & keep_mask
            target = jnp.where(chosen, flat_slots, slot_count).astype(jnp.int32)
            buffer = jnp.zeros((slot_count, D), jnp.float32)
            buffer = buffer.at[target[:, 0]].add(normed2, mode='drop')
            buffer = buffer.at[target[:, 1]].add(normed2, mode='drop')
            buffer = low_back(buffer)
            pre_act = low_back(jnp.dot(buffer, first_w, precision=highest))
            hidden = low(jax.nn.gelu(pre_act, approximate=False))
            result = low(low_back(jnp.dot(hidden, second_w, precision=highest)))
            picked = result[jnp.minimum(target, slot_count - 1)]
            weight = gates * chosen.astype(jnp.float32)
            return (total + lax.optimization_barrier(jnp.sum(weight[:, :, None] * picked, axis=1)), None)
        moe, _ = lax.scan(jax.checkpoint(expert_step), jnp.zeros((TOKENS, D), jnp.float32), (jnp.arange(EXPERTS, dtype=jnp.int32), w_first, w_second))
        return mid + moe
    arrays = (tokens, ln1_gain, ln1_bias, qkv_weight, out_weight, ln2_gain, ln2_bias, router_weight, expert_in, expert_out)
    arrays = tuple((item.astype(jnp.float32) for item in arrays))
    output, pullback = jax.vjp(forward, *arrays)
    grads = pullback(cotangent.astype(jnp.float32))
    return (output.astype(jnp.bfloat16), grads[0], grads[1], grads[2], grads[3], grads[4], grads[5], grads[6], grads[7], grads[8], grads[9])
```

```python
import functools

import jax
import jax.numpy as jnp
from jax import lax
from jax.experimental import pallas as pl
from jax.experimental.pallas import tpu as pltpu
from jax.sharding import PartitionSpec as P

HEADS = 12
HEAD = 64
TOP = 2
SEQ = 197
SEQ_PAD = 208
PAIR = 2 * HEAD


epsilon = 1e-06


def layer_norm(values, gain, offset):
    centre = jnp.mean(values, axis=-1, keepdims=True)
    centred = values - centre
    spread = jnp.mean(centred * centred, axis=-1, keepdims=True)
    return centred * lax.rsqrt(spread + epsilon) * gain + offset


def gelu_and_slope(values):
    size = jnp.abs(values) * 0.7071067811865476
    step = 1.0 / (1.0 + 0.3275911 * size)
    decay = jnp.exp(-(size * size))
    poly = step * (
        0.254829592
        + step * (-0.284496736 + step * (1.421413741 + step * (-1.453152027 + step * 1.061405429)))
    )
    tail = 0.5 * poly * decay
    cdf = jnp.where(values < 0, tail, 1.0 - tail)
    return values * cdf, cdf + values * decay * 0.3989422804014327


def matmul_tn(left, right):
    return lax.dot_general(
        left, right, (((0,), (0,)), ((), ())), preferred_element_type=jnp.float32
    )


def matmul_nt(left, right):
    return lax.dot_general(
        left, right, (((1,), (1,)), ((), ())), preferred_element_type=jnp.float32
    )


def head_lanes(first):
    lanes = lax.broadcasted_iota(jnp.int32, (SEQ_PAD, PAIR), 1)
    return (lanes < HEAD) if first else (lanes >= HEAD)


def head_probs(queries, keys):
    scores = matmul_nt(queries, keys) * HEAD ** (-0.5)
    columns = lax.broadcasted_iota(jnp.int32, (SEQ_PAD, SEQ_PAD), 1)
    scores = jnp.where(columns < SEQ, scores, -1e30)
    powers = jnp.exp(scores - jnp.max(scores, axis=-1, keepdims=True))
    return powers * (1.0 / jnp.sum(powers, axis=-1, keepdims=True))


def attend_kernel(width, qkv_ref, out_ref):
    for pair in range(width // PAIR):
        at = pair * PAIR
        queries = qkv_ref[0, :, at : at + PAIR]
        keys = qkv_ref[0, :, width + at : width + at + PAIR]
        values = qkv_ref[0, :, 2 * width + at : 2 * width + at + PAIR]
        result = None
        for first in (True, False):
            lanes = head_lanes(first)
            mine = jnp.where(lanes, queries, jnp.zeros_like(queries))
            probs = head_probs(mine, keys).astype(jnp.bfloat16)
            part = jnp.dot(probs, values, preferred_element_type=jnp.float32)
            result = part if result is None else jnp.where(lanes, part, result)
        out_ref[0, :, at : at + PAIR] = result.astype(jnp.bfloat16)


def attend_back_kernel(width, qkv_ref, grad_ref, out_ref):
    scale = HEAD ** (-0.5)
    for pair in range(width // PAIR):
        at = pair * PAIR
        queries = qkv_ref[0, :, at : at + PAIR]
        keys = qkv_ref[0, :, width + at : width + at + PAIR]
        values = qkv_ref[0, :, 2 * width + at : 2 * width + at + PAIR]
        grads = grad_ref[0, :, at : at + PAIR]
        grad_q = grad_k = grad_v = 0.0
        for first in (True, False):
            lanes = head_lanes(first)
            zero = jnp.zeros_like(queries)
            my_q = jnp.where(lanes, queries, zero)
            my_k = jnp.where(lanes, keys, zero)
            my_g = jnp.where(lanes, grads, zero)
            probs = head_probs(my_q, keys)
            grad_v = grad_v + matmul_tn(probs.astype(jnp.bfloat16), my_g)
            grad_p = matmul_nt(my_g, values)
            inner = jnp.sum(grad_p * probs, axis=-1, keepdims=True)
            grad_s = (probs * (grad_p - inner)).astype(jnp.bfloat16)
            grad_q = grad_q + jnp.dot(grad_s, my_k, preferred_element_type=jnp.float32)
            grad_k = grad_k + matmul_tn(grad_s, my_q)
        out_ref[0, :, at : at + PAIR] = (grad_q * scale).astype(jnp.bfloat16)
        out_ref[0, :, width + at : width + at + PAIR] = (grad_k * scale).astype(jnp.bfloat16)
        out_ref[0, :, 2 * width + at : 2 * width + at + PAIR] = grad_v.astype(jnp.bfloat16)


def per_image(kernel, columns, n_images, flops, *arrays):
    return pl.pallas_call(
        kernel,
        grid=(n_images,),
        in_specs=[
            pl.BlockSpec((1, SEQ_PAD, array.shape[2]), lambda i: (i, 0, 0)) for array in arrays
        ],
        out_specs=pl.BlockSpec((1, SEQ_PAD, columns), lambda i: (i, 0, 0)),
        out_shape=jax.ShapeDtypeStruct((n_images, SEQ_PAD, columns), jnp.bfloat16),
        compiler_params=pltpu.CompilerParams(vmem_limit_bytes=24 * 1024 * 1024),
        cost_estimate=pl.CostEstimate(
            flops=flops, bytes_accessed=8_000_000, transcendentals=2_000_000
        ),
    )(*arrays)


def pad_rows(values, n_images, fill=0):
    columns = values.shape[1]
    split = values.reshape(n_images, SEQ, columns)
    split = jnp.pad(split, ((0, 0), (0, SEQ_PAD - SEQ), (0, 0)), constant_values=fill)
    return split.reshape(n_images * SEQ_PAD, columns)


def unpad_rows(values, n_images):
    columns = values.shape[1]
    split = values.reshape(n_images, SEQ_PAD, columns)[:, :SEQ]
    return split.reshape(n_images * SEQ, columns)


def pad_columns(parts, multiple):
    total = sum(part.shape[1] for part in parts)
    extra = -total % multiple
    if extra:
        parts = parts + [jnp.zeros((parts[0].shape[0], extra), parts[0].dtype)]
    return jnp.concatenate(parts, axis=1)


SWAP = [(0, 1), (1, 0)]


def sum_replicas(grad):
    low = lax.optimization_barrier(grad.astype(jnp.bfloat16))
    if lax.axis_size("rep") == 2:
        other = lax.ppermute(low, "rep", SWAP)
        return low.astype(jnp.float32) + other.astype(jnp.float32)
    return lax.psum(low, "rep").astype(jnp.float32)


def sum_shared(parts):
    grad = pad_columns(parts, 256)
    rows, columns = grad.shape
    owners = lax.axis_size("exp")
    if lax.axis_size("rep") != 2:
        share = lax.psum_scatter(grad, "exp", scatter_dimension=0, tiled=True)
        return lax.psum(share.astype(jnp.bfloat16), "rep").astype(jnp.float32)
    half = columns // 2
    low = grad.astype(jnp.bfloat16)
    is_first = lax.axis_index("rep") == 0
    left, right = low[:, :half], low[:, half:]
    received = lax.ppermute(jnp.where(is_first, right, left), "rep", SWAP)
    kept = jnp.where(is_first, left, right)
    both = (kept.astype(jnp.float32) + received.astype(jnp.float32)).astype(jnp.bfloat16)
    landed = lax.all_to_all(
        both.reshape(owners, rows // owners, half), "exp", split_axis=0, concat_axis=0, tiled=True
    )
    mine = lax.optimization_barrier(jnp.sum(landed.astype(jnp.float32), axis=0))
    other = lax.ppermute(mine, "rep", SWAP)
    return jnp.concatenate(
        [jnp.where(is_first, mine, other), jnp.where(is_first, other, mine)], axis=1
    )


def on_device(
    tokens,
    ln1_gain,
    ln1_bias,
    qkv_weight,
    out_weight,
    ln2_gain,
    ln2_bias,
    router_weight,
    expert_in,
    expert_out,
    expert_ids,
    slot_ids,
    dropped,
    cotangent,
):
    tok_rows, width = tokens.shape
    n_images = tok_rows // SEQ
    rows = n_images * SEQ_PAD
    local_experts = expert_in.shape[0]
    exp_devices = lax.axis_size("exp")
    num_experts = exp_devices * local_experts
    capacity = (5 * TOP * tok_rows // (4 * num_experts) + 7) // 8 * 8
    slot_total = num_experts * capacity

    def exchange(slots):
        return lax.all_to_all(
            slots.reshape(num_experts, capacity, -1), "exp", split_axis=0, concat_axis=0, tiled=True
        )

    def to_expert(slots):
        arrived = exchange(slots).reshape(exp_devices, local_experts, capacity, -1)
        return arrived.transpose(1, 0, 2, 3).reshape(local_experts, exp_devices * capacity, -1)

    def to_tokens(results):
        outgoing = results.reshape(local_experts, exp_devices, capacity, -1).transpose(1, 0, 2, 3)
        return exchange(outgoing).reshape(slot_total, -1)

    packed = pad_columns(
        [
            qkv_weight,
            out_weight,
            router_weight,
            ln1_gain[:, None],
            ln1_bias[:, None],
            ln2_gain[:, None],
            ln2_bias[:, None],
        ],
        128,
    )
    gathered = lax.all_gather(packed, "exp", axis=0, tiled=True)
    w_qkv = gathered[:, : 3 * width]
    w_attn = gathered[:, 3 * width : 4 * width]
    at = 4 * width + num_experts
    w_router = gathered[:, 4 * width : at]
    norms = gathered[:, at : at + 4].astype(jnp.float32)
    gain_one, bias_one, gain_two, bias_two = (norms[:, i] for i in range(4))

    targets = jnp.where(dropped == 1, slot_total, expert_ids * capacity + slot_ids)
    targets = pad_rows(targets, n_images, slot_total)
    ids = pad_rows(expert_ids, n_images)
    keep_mask = (1 - pad_rows(dropped, n_images)).astype(jnp.float32)
    all_slots = jnp.arange(slot_total, dtype=jnp.int32)[None, :]
    in_slot = [targets[:, k : k + 1] == all_slots for k in range(TOP)]
    pick = [hit.astype(jnp.bfloat16) for hit in in_slot]
    pick_any = (in_slot[0] | in_slot[1]).astype(jnp.bfloat16)

    grad_low = pad_rows(cotangent, n_images)
    grad_slots = matmul_tn(pick_any, grad_low).astype(jnp.bfloat16)
    grad_arrived = to_expert(grad_slots)

    inputs = pad_rows(tokens, n_images).astype(jnp.float32)
    normed1 = layer_norm(inputs, gain_one, bias_one).astype(jnp.bfloat16)
    qkv_low = jnp.dot(normed1, w_qkv, preferred_element_type=jnp.float32).astype(jnp.bfloat16)
    qkv_images = qkv_low.reshape(n_images, SEQ_PAD, 3 * width)
    pair_flops = 2 * n_images * HEADS * SEQ_PAD * SEQ_PAD * PAIR
    attended = per_image(
        functools.partial(attend_kernel, width), width, n_images, 2 * pair_flops, qkv_images
    ).reshape(rows, width)
    mid = inputs + jnp.dot(attended, w_attn, preferred_element_type=jnp.float32)
    normed2 = layer_norm(mid, gain_two, bias_two).astype(jnp.bfloat16)
    expert_rows = to_expert(matmul_tn(pick_any, normed2).astype(jnp.bfloat16))
    logits = jnp.dot(normed2, w_router, preferred_element_type=jnp.float32)
    router_probs = jax.nn.softmax(logits, axis=-1)
    onehot = (
        ids[:, :, None] == jnp.arange(num_experts, dtype=jnp.int32)[None, None, :]
    ).astype(jnp.float32)
    gates = jnp.sum(onehot * router_probs[:, None, :], axis=-1) * keep_mask
    gate_slots = sum(
        jnp.sum(jnp.where(in_slot[k], gates[:, k : k + 1], 0.0), axis=0) for k in range(TOP)
    )
    gates_arrived = to_expert(gate_slots)

    pre_act = jnp.einsum("erd,edf->erf", expert_rows, expert_in, preferred_element_type=jnp.float32)
    hidden, slope = gelu_and_slope(pre_act)
    hidden_low = hidden.astype(jnp.bfloat16)
    slope_low = lax.optimization_barrier(slope.astype(jnp.bfloat16))
    result_low = jnp.einsum(
        "erf,efd->erd", hidden_low, expert_out, preferred_element_type=jnp.float32
    ).astype(jnp.bfloat16)
    returned = to_tokens(result_low)
    grad_result = (gates_arrived * grad_arrived.astype(jnp.float32)).astype(jnp.bfloat16)
    grad_hidden = jnp.einsum(
        "erd,efd->erf", grad_result, expert_out, preferred_element_type=jnp.float32
    )
    grad_pre = (grad_hidden * slope_low.astype(jnp.float32)).astype(jnp.bfloat16)
    grad_sent = jnp.einsum(
        "erf,edf->erd", grad_pre, expert_in, preferred_element_type=jnp.float32
    ).astype(jnp.bfloat16)
    grad_home = to_tokens(grad_sent)
    grad_second = jnp.einsum(
        "erf,erd->efd", hidden_low, grad_result, preferred_element_type=jnp.float32
    )
    grad_first = jnp.einsum(
        "erd,erf->edf", expert_rows, grad_pre, preferred_element_type=jnp.float32
    )
    total_second = sum_replicas(grad_second)
    total_first = sum_replicas(grad_first)

    grad_output = grad_low.astype(jnp.float32)
    back_rows = [jnp.dot(pick[k], returned, preferred_element_type=jnp.float32) for k in range(TOP)]
    moe = sum(gates[:, k : k + 1] * back_rows[k] for k in range(TOP))
    mixed = unpad_rows((mid + moe).astype(jnp.bfloat16), n_images)
    grad_gates = jnp.stack(
        [jnp.sum(grad_output * back_rows[k], axis=-1) for k in range(TOP)], axis=1
    )
    grad_chosen = grad_gates * keep_mask
    grad_probs = jnp.sum(onehot * grad_chosen[:, :, None], axis=1)
    inner_probs = jnp.sum(grad_probs * router_probs, axis=-1, keepdims=True)
    grad_logits = (router_probs * (grad_probs - inner_probs)).astype(jnp.bfloat16)
    grad_router = matmul_tn(normed2, grad_logits)
    grad_normed2 = jnp.dot(pick_any, grad_home, preferred_element_type=jnp.float32)
    grad_normed2 = grad_normed2 + matmul_nt(grad_logits, w_router)
    _, norm_two_pull = jax.vjp(layer_norm, mid, gain_two, bias_two)
    grad_mid_part, grad_gain_two, grad_bias_two = norm_two_pull(grad_normed2)
    grad_mid = grad_output + grad_mid_part
    grad_mid_low = grad_mid.astype(jnp.bfloat16)
    grad_attn_w = matmul_tn(attended, grad_mid_low)
    total_early = sum_shared(
        [grad_attn_w, grad_router, grad_gain_two[:, None], grad_bias_two[:, None]]
    )
    grad_attended = matmul_nt(grad_mid_low, w_attn).astype(jnp.bfloat16)
    grad_qkv_rows = per_image(
        functools.partial(attend_back_kernel, width),
        3 * width,
        n_images,
        5 * pair_flops,
        qkv_images,
        grad_attended.reshape(n_images, SEQ_PAD, width),
    ).reshape(rows, 3 * width)
    grad_qkv_w = matmul_tn(normed1, grad_qkv_rows)
    grad_normed1 = matmul_nt(grad_qkv_rows, w_qkv)
    _, norm_one_pull = jax.vjp(layer_norm, inputs, gain_one, bias_one)
    grad_in_part, grad_gain_one, grad_bias_one = norm_one_pull(grad_normed1)
    grad_tokens = unpad_rows(grad_mid + grad_in_part, n_images)
    total_late = sum_shared([grad_qkv_w, grad_gain_one[:, None], grad_bias_one[:, None]])
    at = width + num_experts
    return (
        mixed,
        grad_tokens,
        total_late[:, 3 * width],
        total_late[:, 3 * width + 1],
        total_late[:, : 3 * width],
        total_early[:, :width],
        total_early[:, at],
        total_early[:, at + 1],
        total_early[:, width:at],
        total_first,
        total_second,
    )


def solution(mesh):
    placed = (
        P(("rep", "exp"), None),
        P("exp"),
        P("exp"),
        P("exp", None),
        P("exp", None),
        P("exp"),
        P("exp"),
        P("exp", None),
        P("exp", None, None),
        P("exp", None, None),
        P(("rep", "exp"), None),
        P(("rep", "exp"), None),
        P(("rep", "exp"), None),
        P(("rep", "exp"), None),
    )
    return jax.shard_map(
        on_device,
        mesh=mesh,
        in_specs=placed,
        out_specs=(
            P(("rep", "exp"), None),
            P(("rep", "exp"), None),
            P("exp"),
            P("exp"),
            P("exp", None),
            P("exp", None),
            P("exp"),
            P("exp"),
            P("exp", None),
            P("exp", None, None),
            P("exp", None, None),
        ),
        check_vma=False,
    )
```

```python
import functools

import jax
import jax.numpy as jnp
from jax import lax
from jax.experimental import pallas as pl
from jax.experimental.pallas import tpu as pltpu
from jax.sharding import PartitionSpec as P

HEADS = 12
HEAD = 64
TOP = 2
SEQ = 197
SEQ_PAD = 208
PAIR = 2 * HEAD


epsilon = 1e-06


def layer_norm(values, gain, offset):
    centre = jnp.mean(values, axis=-1, keepdims=True)
    centred = values - centre
    spread = jnp.mean(centred * centred, axis=-1, keepdims=True)
    return centred * lax.rsqrt(spread + epsilon) * gain + offset


def gelu_and_slope(values):
    size = jnp.abs(values) * 0.7071067811865476
    step = 1.0 / (1.0 + 0.3275911 * size)
    decay = jnp.exp(-(size * size))
    poly = step * (
        0.254829592
        + step * (-0.284496736 + step * (1.421413741 + step * (-1.453152027 + step * 1.061405429)))
    )
    tail = 0.5 * poly * decay
    cdf = jnp.where(values < 0, tail, 1.0 - tail)
    return values * cdf, cdf + values * decay * 0.3989422804014327


def matmul_tn(left, right):
    return lax.dot_general(
        left, right, (((0,), (0,)), ((), ())), preferred_element_type=jnp.float32
    )


def matmul_nt(left, right):
    return lax.dot_general(
        left, right, (((1,), (1,)), ((), ())), preferred_element_type=jnp.float32
    )


def head_lanes(first):
    lanes = lax.broadcasted_iota(jnp.int32, (SEQ_PAD, PAIR), 1)
    return (lanes < HEAD) if first else (lanes >= HEAD)


def head_probs(queries, keys):
    scores = matmul_nt(queries, keys) * HEAD ** (-0.5)
    columns = lax.broadcasted_iota(jnp.int32, (SEQ_PAD, SEQ_PAD), 1)
    scores = jnp.where(columns < SEQ, scores, -1e30)
    powers = jnp.exp(scores - jnp.max(scores, axis=-1, keepdims=True))
    return powers * (1.0 / jnp.sum(powers, axis=-1, keepdims=True))


def attend_kernel(width, qkv_ref, out_ref):
    for pair in range(width // PAIR):
        at = pair * PAIR
        queries = qkv_ref[0, :, at : at + PAIR]
        keys = qkv_ref[0, :, width + at : width + at + PAIR]
        values = qkv_ref[0, :, 2 * width + at : 2 * width + at + PAIR]
        result = None
        for first in (True, False):
            lanes = head_lanes(first)
            mine = jnp.where(lanes, queries, jnp.zeros_like(queries))
            probs = head_probs(mine, keys).astype(jnp.bfloat16)
            part = jnp.dot(probs, values, preferred_element_type=jnp.float32)
            result = part if result is None else jnp.where(lanes, part, result)
        out_ref[0, :, at : at + PAIR] = result.astype(jnp.bfloat16)


def attend_back_kernel(width, qkv_ref, grad_ref, out_ref):
    scale = HEAD ** (-0.5)
    for pair in range(width // PAIR):
        at = pair * PAIR
        queries = qkv_ref[0, :, at : at + PAIR]
        keys = qkv_ref[0, :, width + at : width + at + PAIR]
        values = qkv_ref[0, :, 2 * width + at : 2 * width + at + PAIR]
        grads = grad_ref[0, :, at : at + PAIR]
        grad_q = grad_k = grad_v = 0.0
        for first in (True, False):
            lanes = head_lanes(first)
            zero = jnp.zeros_like(queries)
            my_q = jnp.where(lanes, queries, zero)
            my_k = jnp.where(lanes, keys, zero)
            my_g = jnp.where(lanes, grads, zero)
            probs = head_probs(my_q, keys)
            grad_v = grad_v + matmul_tn(probs.astype(jnp.bfloat16), my_g)
            grad_p = matmul_nt(my_g, values)
            inner = jnp.sum(grad_p * probs, axis=-1, keepdims=True)
            grad_s = (probs * (grad_p - inner)).astype(jnp.bfloat16)
            grad_q = grad_q + jnp.dot(grad_s, my_k, preferred_element_type=jnp.float32)
            grad_k = grad_k + matmul_tn(grad_s, my_q)
        out_ref[0, :, at : at + PAIR] = (grad_q * scale).astype(jnp.bfloat16)
        out_ref[0, :, width + at : width + at + PAIR] = (grad_k * scale).astype(jnp.bfloat16)
        out_ref[0, :, 2 * width + at : 2 * width + at + PAIR] = grad_v.astype(jnp.bfloat16)


def per_image(kernel, columns, n_images, flops, *arrays):
    return pl.pallas_call(
        kernel,
        grid=(n_images,),
        in_specs=[
            pl.BlockSpec((1, SEQ_PAD, array.shape[2]), lambda i: (i, 0, 0)) for array in arrays
        ],
        out_specs=pl.BlockSpec((1, SEQ_PAD, columns), lambda i: (i, 0, 0)),
        out_shape=jax.ShapeDtypeStruct((n_images, SEQ_PAD, columns), jnp.bfloat16),
        compiler_params=pltpu.CompilerParams(vmem_limit_bytes=24 * 1024 * 1024),
        cost_estimate=pl.CostEstimate(
            flops=flops, bytes_accessed=8_000_000, transcendentals=2_000_000
        ),
    )(*arrays)


def pad_rows(values, n_images, fill=0):
    columns = values.shape[1]
    split = values.reshape(n_images, SEQ, columns)
    split = jnp.pad(split, ((0, 0), (0, SEQ_PAD - SEQ), (0, 0)), constant_values=fill)
    return split.reshape(n_images * SEQ_PAD, columns)


def unpad_rows(values, n_images):
    columns = values.shape[1]
    split = values.reshape(n_images, SEQ_PAD, columns)[:, :SEQ]
    return split.reshape(n_images * SEQ, columns)


def pad_columns(parts, multiple):
    total = sum(part.shape[1] for part in parts)
    extra = -total % multiple
    if extra:
        parts = parts + [jnp.zeros((parts[0].shape[0], extra), parts[0].dtype)]
    return jnp.concatenate(parts, axis=1)


SWAP = [(0, 1), (1, 0)]


def sum_replicas(grad):
    low = lax.optimization_barrier(grad.astype(jnp.bfloat16))
    if lax.axis_size("rep") == 2:
        other = lax.ppermute(low, "rep", SWAP)
        return low.astype(jnp.float32) + other.astype(jnp.float32)
    return lax.psum(low, "rep").astype(jnp.float32)


def start_shared(left, right, small):
    small = pad_columns(small, 128).astype(jnp.bfloat16)
    if lax.axis_size("rep") != 2:
        grad = jnp.concatenate([matmul_tn(left, right), small.astype(jnp.float32)], axis=1)
        return lax.psum_scatter(grad, "exp", scatter_dimension=0, tiled=True)
    half = right.shape[1] // 2
    place = lax.axis_index("rep")

    def product(which):
        columns = lax.dynamic_slice_in_dim(right, which * half, half, axis=1)
        return matmul_tn(left, columns).astype(jnp.bfloat16)

    received = lax.ppermute(product(1 - place), "rep", SWAP)
    small = lax.optimization_barrier(small)
    small_received = lax.ppermute(small, "rep", SWAP)
    both = product(place).astype(jnp.float32) + received.astype(jnp.float32)
    small_both = small.astype(jnp.float32) + small_received.astype(jnp.float32)
    return jnp.concatenate([both.astype(jnp.bfloat16), small_both.astype(jnp.bfloat16)], axis=1)


def send_shared(both):
    if lax.axis_size("rep") != 2:
        return both
    owners = lax.axis_size("exp")
    parts = both.reshape(owners, both.shape[0] // owners, both.shape[1])
    return lax.all_to_all(parts, "exp", split_axis=0, concat_axis=0, tiled=True)


def finish_shared(landed, columns):
    if lax.axis_size("rep") != 2:
        total = lax.psum(landed.astype(jnp.bfloat16), "rep").astype(jnp.float32)
        return total[:, :columns], total[:, columns:]
    half = columns // 2
    is_first = lax.axis_index("rep") == 0
    mine = lax.optimization_barrier(jnp.sum(landed.astype(jnp.float32), axis=0))
    small = mine[:, half:]
    mine = mine[:, :half]
    other = lax.ppermute(mine, "rep", SWAP)
    large = jnp.concatenate(
        [jnp.where(is_first, mine, other), jnp.where(is_first, other, mine)], axis=1
    )
    return large, small


def on_device(
    tokens,
    ln1_gain,
    ln1_bias,
    qkv_weight,
    out_weight,
    ln2_gain,
    ln2_bias,
    router_weight,
    expert_in,
    expert_out,
    expert_ids,
    slot_ids,
    dropped,
    cotangent,
):
    tok_rows, width = tokens.shape
    n_images = tok_rows // SEQ
    rows = n_images * SEQ_PAD
    local_experts = expert_in.shape[0]
    exp_devices = lax.axis_size("exp")
    num_experts = exp_devices * local_experts
    capacity = (5 * TOP * tok_rows // (4 * num_experts) + 7) // 8 * 8
    slot_total = num_experts * capacity

    def exchange(slots):
        return lax.all_to_all(
            slots.reshape(num_experts, capacity, -1), "exp", split_axis=0, concat_axis=0, tiled=True
        )

    def to_expert(slots):
        arrived = exchange(slots).reshape(exp_devices, local_experts, capacity, -1)
        return arrived.transpose(1, 0, 2, 3).reshape(local_experts, exp_devices * capacity, -1)

    def to_tokens(results):
        outgoing = results.reshape(local_experts, exp_devices, capacity, -1).transpose(1, 0, 2, 3)
        return exchange(outgoing).reshape(slot_total, -1)

    packed = pad_columns(
        [
            qkv_weight,
            out_weight,
            router_weight,
            jnp.stack([ln1_gain, ln1_bias, ln2_gain, ln2_bias], axis=1),
        ],
        128,
    )
    gathered = lax.all_gather(packed, "exp", axis=0, tiled=True)
    targets = jnp.where(dropped == 1, slot_total, expert_ids * capacity + slot_ids)
    targets = pad_rows(targets, n_images, slot_total)
    ids = pad_rows(expert_ids, n_images)
    keep_mask = (1 - pad_rows(dropped, n_images)).astype(jnp.float32)
    all_slots = jnp.arange(slot_total, dtype=jnp.int32)[None, :]
    in_slot = [targets[:, k : k + 1] == all_slots for k in range(TOP)]
    pick = [hit.astype(jnp.bfloat16) for hit in in_slot]
    pick_any = (in_slot[0] | in_slot[1]).astype(jnp.bfloat16)
    grad_low = pad_rows(cotangent, n_images)
    grad_slots = matmul_tn(pick_any, grad_low).astype(jnp.bfloat16)
    gathered, grad_arrived = lax.optimization_barrier((gathered, to_expert(grad_slots)))

    w_qkv = gathered[:, : 3 * width]
    w_attn = gathered[:, 3 * width : 4 * width]
    at = 4 * width + num_experts
    w_router = gathered[:, 4 * width : at]
    norms = gathered[:, at : at + 4].astype(jnp.float32)
    gain_one, bias_one, gain_two, bias_two = (norms[:, i] for i in range(4))

    inputs = pad_rows(tokens, n_images).astype(jnp.float32)
    normed1 = layer_norm(inputs, gain_one, bias_one).astype(jnp.bfloat16)
    qkv_low = jnp.dot(normed1, w_qkv, preferred_element_type=jnp.float32).astype(jnp.bfloat16)
    qkv_images = qkv_low.reshape(n_images, SEQ_PAD, 3 * width)
    attended = per_image(
        functools.partial(attend_kernel, width), width, n_images, 8_000_000_000, qkv_images
    ).reshape(rows, width)
    mid = inputs + jnp.dot(attended, w_attn, preferred_element_type=jnp.float32)
    normed2 = layer_norm(mid, gain_two, bias_two).astype(jnp.bfloat16)
    expert_rows = to_expert(matmul_tn(pick_any, normed2).astype(jnp.bfloat16))
    logits = jnp.dot(normed2, w_router, preferred_element_type=jnp.float32)
    router_probs = jax.nn.softmax(logits, axis=-1)
    onehot = (
        ids[:, :, None] == jnp.arange(num_experts, dtype=jnp.int32)[None, None, :]
    ).astype(jnp.float32)
    gates = jnp.sum(onehot * router_probs[:, None, :], axis=-1) * keep_mask
    own = lax.axis_index("exp") * local_experts + jnp.arange(local_experts, dtype=jnp.int32)
    own_column = own[:, None, None] == jnp.arange(num_experts, dtype=jnp.int32)[None, None, :]
    slot_probs = jax.nn.softmax(
        jnp.einsum("erd,dn->ern", expert_rows, w_router, preferred_element_type=jnp.float32),
        axis=-1,
    )
    gates_arrived = jnp.sum(jnp.where(own_column, slot_probs, 0.0), axis=-1, keepdims=True)

    pre_act = jnp.einsum("erd,edf->erf", expert_rows, expert_in, preferred_element_type=jnp.float32)
    hidden, slope = gelu_and_slope(pre_act)
    hidden_low = hidden.astype(jnp.bfloat16)
    slope_low = lax.optimization_barrier(slope.astype(jnp.bfloat16))
    result_low = jnp.einsum(
        "erf,efd->erd", hidden_low, expert_out, preferred_element_type=jnp.float32
    ).astype(jnp.bfloat16)
    returned = to_tokens(result_low)
    grad_result = (gates_arrived * grad_arrived.astype(jnp.float32)).astype(jnp.bfloat16)
    grad_hidden = jnp.einsum(
        "erd,efd->erf", grad_result, expert_out, preferred_element_type=jnp.float32
    )
    grad_pre = (grad_hidden * slope_low.astype(jnp.float32)).astype(jnp.bfloat16)
    grad_sent = jnp.einsum(
        "erf,edf->erd", grad_pre, expert_in, preferred_element_type=jnp.float32
    ).astype(jnp.bfloat16)
    grad_home = to_tokens(grad_sent)
    grad_second = jnp.einsum(
        "erf,erd->efd", hidden_low, grad_result, preferred_element_type=jnp.float32
    )
    grad_first = jnp.einsum(
        "erd,erf->edf", expert_rows, grad_pre, preferred_element_type=jnp.float32
    )
    total_second = sum_replicas(grad_second)
    total_first = sum_replicas(grad_first)

    grad_output = grad_low.astype(jnp.float32)
    back_rows = [jnp.dot(pick[k], returned, preferred_element_type=jnp.float32) for k in range(TOP)]
    moe = sum(gates[:, k : k + 1] * back_rows[k] for k in range(TOP))
    mixed = unpad_rows((mid + moe).astype(jnp.bfloat16), n_images)
    grad_gates = jnp.stack(
        [jnp.sum(grad_output * back_rows[k], axis=-1) for k in range(TOP)], axis=1
    )
    grad_chosen = grad_gates * keep_mask
    grad_probs = jnp.sum(onehot * grad_chosen[:, :, None], axis=1)
    inner_probs = jnp.sum(grad_probs * router_probs, axis=-1, keepdims=True)
    grad_logits = (router_probs * (grad_probs - inner_probs)).astype(jnp.bfloat16)
    grad_router = matmul_tn(normed2, grad_logits)
    grad_normed2 = jnp.dot(pick_any, grad_home, preferred_element_type=jnp.float32)
    grad_normed2 = grad_normed2 + matmul_nt(grad_logits, w_router)
    _, norm_two_pull = jax.vjp(layer_norm, mid, gain_two, bias_two)
    grad_mid_part, grad_gain_two, grad_bias_two = norm_two_pull(grad_normed2)
    grad_mid = grad_output + grad_mid_part
    grad_mid_low = grad_mid.astype(jnp.bfloat16)
    early = start_shared(
        attended,
        grad_mid_low,
        [grad_router, jnp.stack([grad_gain_two, grad_bias_two], axis=1)],
    )
    grad_attended = matmul_nt(grad_mid_low, w_attn).astype(jnp.bfloat16)
    early, grad_attended = lax.optimization_barrier((early, grad_attended))
    early_landed = send_shared(early)
    grad_qkv_rows = per_image(
        functools.partial(attend_back_kernel, width),
        3 * width,
        n_images,
        20_000_000_000,
        qkv_images,
        grad_attended.reshape(n_images, SEQ_PAD, width),
    ).reshape(rows, 3 * width)
    early_landed, grad_qkv_rows = lax.optimization_barrier((early_landed, grad_qkv_rows))
    out_total, early_small = finish_shared(early_landed, width)
    grad_normed1 = matmul_nt(grad_qkv_rows, w_qkv)
    _, norm_one_pull = jax.vjp(layer_norm, inputs, gain_one, bias_one)
    grad_in_part, grad_gain_one, grad_bias_one = norm_one_pull(grad_normed1)
    grad_tokens = unpad_rows(grad_mid + grad_in_part, n_images)
    late = start_shared(
        normed1, grad_qkv_rows, [jnp.stack([grad_gain_one, grad_bias_one], axis=1)]
    )
    qkv_total, late_small = finish_shared(send_shared(late), 3 * width)
    return (
        mixed,
        grad_tokens,
        late_small[:, 0],
        late_small[:, 1],
        qkv_total,
        out_total,
        early_small[:, num_experts],
        early_small[:, num_experts + 1],
        early_small[:, :num_experts],
        total_first,
        total_second,
    )


def solution(mesh):
    placed = (
        P(("rep", "exp"), None),
        P("exp"),
        P("exp"),
        P("exp", None),
        P("exp", None),
        P("exp"),
        P("exp"),
        P("exp", None),
        P("exp", None, None),
        P("exp", None, None),
        P(("rep", "exp"), None),
        P(("rep", "exp"), None),
        P(("rep", "exp"), None),
        P(("rep", "exp"), None),
    )
    return jax.shard_map(
        on_device,
        mesh=mesh,
        in_specs=placed,
        out_specs=(
            P(("rep", "exp"), None),
            P(("rep", "exp"), None),
            P("exp"),
            P("exp"),
            P("exp", None),
            P("exp", None),
            P("exp"),
            P("exp"),
            P("exp", None),
            P("exp", None, None),
            P("exp", None, None),
        ),
        check_vma=False,
    )
```

```python
import functools

import jax
import jax.numpy as jnp
from jax import lax
from jax.experimental import pallas as pl
from jax.experimental.pallas import tpu as pltpu
from jax.sharding import PartitionSpec as P

HEADS = 12
HEAD = 64
TOP = 2
SEQ = 197
SEQ_PAD = 208
PAIR = 2 * HEAD


epsilon = 1e-06


def layer_norm(values, gain, offset):
    centre = jnp.mean(values, axis=-1, keepdims=True)
    centred = values - centre
    spread = jnp.mean(centred * centred, axis=-1, keepdims=True)
    return centred * lax.rsqrt(spread + epsilon) * gain + offset


def gelu_and_slope(values):
    size = jnp.abs(values) * 0.7071067811865476
    step = 1.0 / (1.0 + 0.3275911 * size)
    decay = jnp.exp(-(size * size))
    poly = step * (
        0.254829592
        + step * (-0.284496736 + step * (1.421413741 + step * (-1.453152027 + step * 1.061405429)))
    )
    tail = 0.5 * poly * decay
    cdf = jnp.where(values < 0, tail, 1.0 - tail)
    return values * cdf, cdf + values * decay * 0.3989422804014327


def matmul_tn(left, right):
    return lax.dot_general(
        left, right, (((0,), (0,)), ((), ())), preferred_element_type=jnp.float32
    )


def matmul_nt(left, right):
    return lax.dot_general(
        left, right, (((1,), (1,)), ((), ())), preferred_element_type=jnp.float32
    )


def head_lanes(first):
    lanes = lax.broadcasted_iota(jnp.int32, (SEQ_PAD, PAIR), 1)
    return (lanes < HEAD) if first else (lanes >= HEAD)


def head_probs(queries, keys):
    scores = matmul_nt(queries, keys) * HEAD ** (-0.5)
    columns = lax.broadcasted_iota(jnp.int32, (SEQ_PAD, SEQ_PAD), 1)
    scores = jnp.where(columns < SEQ, scores, -1e30)
    powers = jnp.exp(scores - jnp.max(scores, axis=-1, keepdims=True))
    return powers * (1.0 / jnp.sum(powers, axis=-1, keepdims=True))


def attend_kernel(width, qkv_ref, out_ref):
    for pair in range(width // PAIR):
        at = pair * PAIR
        queries = qkv_ref[0, :, at : at + PAIR]
        keys = qkv_ref[0, :, width + at : width + at + PAIR]
        values = qkv_ref[0, :, 2 * width + at : 2 * width + at + PAIR]
        result = None
        for first in (True, False):
            lanes = head_lanes(first)
            mine = jnp.where(lanes, queries, jnp.zeros_like(queries))
            probs = head_probs(mine, keys).astype(jnp.bfloat16)
            part = jnp.dot(probs, values, preferred_element_type=jnp.float32)
            result = part if result is None else jnp.where(lanes, part, result)
        out_ref[0, :, at : at + PAIR] = result.astype(jnp.bfloat16)


def attend_back_kernel(width, qkv_ref, grad_ref, out_ref):
    scale = HEAD ** (-0.5)
    for pair in range(width // PAIR):
        at = pair * PAIR
        queries = qkv_ref[0, :, at : at + PAIR]
        keys = qkv_ref[0, :, width + at : width + at + PAIR]
        values = qkv_ref[0, :, 2 * width + at : 2 * width + at + PAIR]
        grads = grad_ref[0, :, at : at + PAIR]
        grad_q = grad_k = grad_v = 0.0
        for first in (True, False):
            lanes = head_lanes(first)
            zero = jnp.zeros_like(queries)
            my_q = jnp.where(lanes, queries, zero)
            my_k = jnp.where(lanes, keys, zero)
            my_g = jnp.where(lanes, grads, zero)
            probs = head_probs(my_q, keys)
            grad_v = grad_v + matmul_tn(probs.astype(jnp.bfloat16), my_g)
            grad_p = matmul_nt(my_g, values)
            inner = jnp.sum(grad_p * probs, axis=-1, keepdims=True)
            grad_s = (probs * (grad_p - inner)).astype(jnp.bfloat16)
            grad_q = grad_q + jnp.dot(grad_s, my_k, preferred_element_type=jnp.float32)
            grad_k = grad_k + matmul_tn(grad_s, my_q)
        out_ref[0, :, at : at + PAIR] = (grad_q * scale).astype(jnp.bfloat16)
        out_ref[0, :, width + at : width + at + PAIR] = (grad_k * scale).astype(jnp.bfloat16)
        out_ref[0, :, 2 * width + at : 2 * width + at + PAIR] = grad_v.astype(jnp.bfloat16)


def per_image(kernel, columns, n_images, flops, *arrays):
    return pl.pallas_call(
        kernel,
        grid=(n_images,),
        in_specs=[
            pl.BlockSpec((1, SEQ_PAD, array.shape[2]), lambda i: (i, 0, 0)) for array in arrays
        ],
        out_specs=pl.BlockSpec((1, SEQ_PAD, columns), lambda i: (i, 0, 0)),
        out_shape=jax.ShapeDtypeStruct((n_images, SEQ_PAD, columns), jnp.bfloat16),
        compiler_params=pltpu.CompilerParams(vmem_limit_bytes=24 * 1024 * 1024),
        cost_estimate=pl.CostEstimate(
            flops=flops, bytes_accessed=8_000_000, transcendentals=2_000_000
        ),
    )(*arrays)


def pad_rows(values, n_images, fill=0):
    columns = values.shape[1]
    split = values.reshape(n_images, SEQ, columns)
    split = jnp.pad(split, ((0, 0), (0, SEQ_PAD - SEQ), (0, 0)), constant_values=fill)
    return split.reshape(n_images * SEQ_PAD, columns)


def unpad_rows(values, n_images):
    columns = values.shape[1]
    split = values.reshape(n_images, SEQ_PAD, columns)[:, :SEQ]
    return split.reshape(n_images * SEQ, columns)


def pad_columns(parts, multiple):
    total = sum(part.shape[1] for part in parts)
    extra = -total % multiple
    if extra:
        parts = parts + [jnp.zeros((parts[0].shape[0], extra), parts[0].dtype)]
    return jnp.concatenate(parts, axis=1)


SWAP = [(0, 1), (1, 0)]


def sum_replicas(grad):
    low = lax.optimization_barrier(grad.astype(jnp.bfloat16))
    if lax.axis_size("rep") == 2:
        other = lax.ppermute(low, "rep", SWAP)
        return low.astype(jnp.float32) + other.astype(jnp.float32)
    return lax.psum(low, "rep").astype(jnp.float32)


def start_shared(left, right, small):
    small = pad_columns(small, 128).astype(jnp.bfloat16)
    if lax.axis_size("rep") != 2:
        grad = jnp.concatenate([matmul_tn(left, right), small.astype(jnp.float32)], axis=1)
        return lax.psum_scatter(grad, "exp", scatter_dimension=0, tiled=True)
    half = right.shape[1] // 2
    place = lax.axis_index("rep")

    def product(which):
        columns = lax.dynamic_slice_in_dim(right, which * half, half, axis=1)
        return matmul_tn(left, columns).astype(jnp.bfloat16)

    received = lax.ppermute(product(1 - place), "rep", SWAP)
    small = lax.optimization_barrier(small)
    small_received = lax.ppermute(small, "rep", SWAP)
    both = product(place).astype(jnp.float32) + received.astype(jnp.float32)
    small_both = small.astype(jnp.float32) + small_received.astype(jnp.float32)
    return jnp.concatenate([both.astype(jnp.bfloat16), small_both.astype(jnp.bfloat16)], axis=1)


def send_shared(both):
    if lax.axis_size("rep") != 2:
        return both
    owners = lax.axis_size("exp")
    parts = both.reshape(owners, both.shape[0] // owners, both.shape[1])
    return lax.all_to_all(parts, "exp", split_axis=0, concat_axis=0, tiled=True)


def finish_shared(landed, columns):
    if lax.axis_size("rep") != 2:
        total = lax.psum(landed.astype(jnp.bfloat16), "rep").astype(jnp.float32)
        return total[:, :columns], total[:, columns:]
    half = columns // 2
    is_first = lax.axis_index("rep") == 0
    mine = lax.optimization_barrier(jnp.sum(landed.astype(jnp.float32), axis=0))
    small = mine[:, half:]
    mine = mine[:, :half]
    other = lax.ppermute(mine, "rep", SWAP)
    large = jnp.concatenate(
        [jnp.where(is_first, mine, other), jnp.where(is_first, other, mine)], axis=1
    )
    return large, small


def on_device(
    tokens,
    ln1_gain,
    ln1_bias,
    qkv_weight,
    out_weight,
    ln2_gain,
    ln2_bias,
    router_weight,
    expert_in,
    expert_out,
    expert_ids,
    slot_ids,
    dropped,
    cotangent,
):
    tok_rows, width = tokens.shape
    n_images = tok_rows // SEQ
    rows = n_images * SEQ_PAD
    local_experts = expert_in.shape[0]
    exp_devices = lax.axis_size("exp")
    num_experts = exp_devices * local_experts
    capacity = (5 * TOP * tok_rows // (4 * num_experts) + 7) // 8 * 8
    slot_total = num_experts * capacity

    def exchange(slots):
        return lax.all_to_all(
            slots.reshape(num_experts, capacity, -1), "exp", split_axis=0, concat_axis=0, tiled=True
        )

    def to_expert(slots):
        arrived = exchange(slots).reshape(exp_devices, local_experts, capacity, -1)
        return arrived.transpose(1, 0, 2, 3).reshape(local_experts, exp_devices * capacity, -1)

    def to_tokens(results):
        outgoing = results.reshape(local_experts, exp_devices, capacity, -1).transpose(1, 0, 2, 3)
        return exchange(outgoing).reshape(slot_total, -1)

    packed = pad_columns(
        [
            qkv_weight,
            out_weight,
            router_weight,
            jnp.stack([ln1_gain, ln1_bias, ln2_gain, ln2_bias], axis=1),
        ],
        128,
    )
    gathered = lax.all_gather(packed, "exp", axis=0, tiled=True)
    targets = jnp.where(dropped == 1, slot_total, expert_ids * capacity + slot_ids)
    targets = pad_rows(targets, n_images, slot_total)
    ids = pad_rows(expert_ids, n_images)
    keep_mask = (1 - pad_rows(dropped, n_images)).astype(jnp.float32)
    all_slots = jnp.arange(slot_total, dtype=jnp.int32)[None, :]
    in_slot = [targets[:, k : k + 1] == all_slots for k in range(TOP)]
    pick = [hit.astype(jnp.bfloat16) for hit in in_slot]
    pick_any = (in_slot[0] | in_slot[1]).astype(jnp.bfloat16)
    grad_low = pad_rows(cotangent, n_images)
    grad_slots = matmul_tn(pick_any, grad_low).astype(jnp.bfloat16)

    w_qkv = gathered[:, : 3 * width]
    w_attn = gathered[:, 3 * width : 4 * width]
    at = 4 * width + num_experts
    w_router = gathered[:, 4 * width : at]
    norms = gathered[:, at : at + 4].astype(jnp.float32)
    gain_one, bias_one, gain_two, bias_two = (norms[:, i] for i in range(4))

    inputs = pad_rows(tokens, n_images).astype(jnp.float32)
    normed1 = layer_norm(inputs, gain_one, bias_one).astype(jnp.bfloat16)
    qkv_low = jnp.dot(normed1, w_qkv, preferred_element_type=jnp.float32).astype(jnp.bfloat16)
    qkv_images = qkv_low.reshape(n_images, SEQ_PAD, 3 * width)
    attended = per_image(
        functools.partial(attend_kernel, width), width, n_images, 8_000_000_000, qkv_images
    ).reshape(rows, width)
    mid = inputs + jnp.dot(attended, w_attn, preferred_element_type=jnp.float32)
    normed2 = layer_norm(mid, gain_two, bias_two).astype(jnp.bfloat16)
    expert_rows = to_expert(matmul_tn(pick_any, normed2).astype(jnp.bfloat16))
    expert_rows, grad_slots = lax.optimization_barrier((expert_rows, grad_slots))
    grad_arrived = to_expert(grad_slots)
    logits = jnp.dot(normed2, w_router, preferred_element_type=jnp.float32)
    router_probs = jax.nn.softmax(logits, axis=-1)
    onehot = (
        ids[:, :, None] == jnp.arange(num_experts, dtype=jnp.int32)[None, None, :]
    ).astype(jnp.float32)
    gates = jnp.sum(onehot * router_probs[:, None, :], axis=-1) * keep_mask
    own = lax.axis_index("exp") * local_experts + jnp.arange(local_experts, dtype=jnp.int32)
    own_column = own[:, None, None] == jnp.arange(num_experts, dtype=jnp.int32)[None, None, :]
    slot_probs = jax.nn.softmax(
        jnp.einsum("erd,dn->ern", expert_rows, w_router, preferred_element_type=jnp.float32),
        axis=-1,
    )
    gates_arrived = jnp.sum(jnp.where(own_column, slot_probs, 0.0), axis=-1, keepdims=True)

    pre_act = jnp.einsum("erd,edf->erf", expert_rows, expert_in, preferred_element_type=jnp.float32)
    hidden, slope = gelu_and_slope(pre_act)
    hidden_low = hidden.astype(jnp.bfloat16)
    slope_low = lax.optimization_barrier(slope.astype(jnp.bfloat16))
    result_low = jnp.einsum(
        "erf,efd->erd", hidden_low, expert_out, preferred_element_type=jnp.float32
    ).astype(jnp.bfloat16)
    result_low, grad_arrived = lax.optimization_barrier((result_low, grad_arrived))
    returned = to_tokens(result_low)
    grad_result = (gates_arrived * grad_arrived.astype(jnp.float32)).astype(jnp.bfloat16)
    grad_hidden = jnp.einsum(
        "erd,efd->erf", grad_result, expert_out, preferred_element_type=jnp.float32
    )
    grad_pre = (grad_hidden * slope_low.astype(jnp.float32)).astype(jnp.bfloat16)
    grad_sent = jnp.einsum(
        "erf,edf->erd", grad_pre, expert_in, preferred_element_type=jnp.float32
    ).astype(jnp.bfloat16)
    grad_home = to_tokens(grad_sent)
    grad_second = jnp.einsum(
        "erf,erd->efd", hidden_low, grad_result, preferred_element_type=jnp.float32
    )
    grad_first = jnp.einsum(
        "erd,erf->edf", expert_rows, grad_pre, preferred_element_type=jnp.float32
    )
    total_second = sum_replicas(grad_second)
    total_first = sum_replicas(grad_first)

    grad_output = grad_low.astype(jnp.float32)
    back_rows = [jnp.dot(pick[k], returned, preferred_element_type=jnp.float32) for k in range(TOP)]
    moe = sum(gates[:, k : k + 1] * back_rows[k] for k in range(TOP))
    mixed = unpad_rows((mid + moe).astype(jnp.bfloat16), n_images)
    grad_gates = jnp.stack(
        [jnp.sum(grad_output * back_rows[k], axis=-1) for k in range(TOP)], axis=1
    )
    grad_chosen = grad_gates * keep_mask
    grad_probs = jnp.sum(onehot * grad_chosen[:, :, None], axis=1)
    inner_probs = jnp.sum(grad_probs * router_probs, axis=-1, keepdims=True)
    grad_logits = (router_probs * (grad_probs - inner_probs)).astype(jnp.bfloat16)
    grad_router = matmul_tn(normed2, grad_logits)
    grad_normed2 = jnp.dot(pick_any, grad_home, preferred_element_type=jnp.float32)
    grad_normed2 = grad_normed2 + matmul_nt(grad_logits, w_router)
    _, norm_two_pull = jax.vjp(layer_norm, mid, gain_two, bias_two)
    grad_mid_part, grad_gain_two, grad_bias_two = norm_two_pull(grad_normed2)
    grad_mid = grad_output + grad_mid_part
    grad_mid_low = grad_mid.astype(jnp.bfloat16)
    early = start_shared(
        attended,
        grad_mid_low,
        [grad_router, jnp.stack([grad_gain_two, grad_bias_two], axis=1)],
    )
    grad_attended = matmul_nt(grad_mid_low, w_attn).astype(jnp.bfloat16)
    early, grad_attended = lax.optimization_barrier((early, grad_attended))
    early_landed = send_shared(early)
    grad_qkv_rows = per_image(
        functools.partial(attend_back_kernel, width),
        3 * width,
        n_images,
        20_000_000_000,
        qkv_images,
        grad_attended.reshape(n_images, SEQ_PAD, width),
    ).reshape(rows, 3 * width)
    early_landed, grad_qkv_rows = lax.optimization_barrier((early_landed, grad_qkv_rows))
    out_total, early_small = finish_shared(early_landed, width)
    grad_normed1 = matmul_nt(grad_qkv_rows, w_qkv)
    _, norm_one_pull = jax.vjp(layer_norm, inputs, gain_one, bias_one)
    grad_in_part, grad_gain_one, grad_bias_one = norm_one_pull(grad_normed1)
    grad_tokens = unpad_rows(grad_mid + grad_in_part, n_images)
    late = start_shared(
        normed1, grad_qkv_rows, [jnp.stack([grad_gain_one, grad_bias_one], axis=1)]
    )
    qkv_total, late_small = finish_shared(send_shared(late), 3 * width)
    return (
        mixed,
        grad_tokens,
        late_small[:, 0],
        late_small[:, 1],
        qkv_total,
        out_total,
        early_small[:, num_experts],
        early_small[:, num_experts + 1],
        early_small[:, :num_experts],
        total_first,
        total_second,
    )


def solution(mesh):
    placed = (
        P(("rep", "exp"), None),
        P("exp"),
        P("exp"),
        P("exp", None),
        P("exp", None),
        P("exp"),
        P("exp"),
        P("exp", None),
        P("exp", None, None),
        P("exp", None, None),
        P(("rep", "exp"), None),
        P(("rep", "exp"), None),
        P(("rep", "exp"), None),
        P(("rep", "exp"), None),
    )
    return jax.shard_map(
        on_device,
        mesh=mesh,
        in_specs=placed,
        out_specs=(
            P(("rep", "exp"), None),
            P(("rep", "exp"), None),
            P("exp"),
            P("exp"),
            P("exp", None),
            P("exp", None),
            P("exp"),
            P("exp"),
            P("exp", None),
            P("exp", None, None),
            P("exp", None, None),
        ),
        check_vma=False,
    )
```
